32 devices in a mesh: dp: 2 (over x), row: 4 (over z), col: 4 (over y, core).
Axes of the slice: x: 2, y: 2, z: 4, core: 2. Of those that a mesh axis runs over, the one named last changes fastest.
Arguments:
- block_in: bfloat16 [4096, 1088], P(('dp', 'col'), 'row'), may hold values from -6 to 6
- cotangent: bfloat16 [4096, 1088], P(('dp', 'col'), 'row'), may hold values from -0.0390625 to 0.0390625
- lengths: int32 [8, 3], P(('dp', 'row')), may hold values from 1 to 384, 512 in all within a row
- qkv_weight: float32 [1088, 4, 816], P('row', 'col', 'dp'), may hold values from -0.1875 to 0.1875
- proj_weight: float32 [1088, 4, 272], P('col', 'row', 'dp'), may hold values from -1.5 to 1.5
- fc1_weight: float32 [1088, 4, 1088], P('row', 'col', 'dp'), may hold values from -0.25 to 0.25
- fc2_weight: float32 [4352, 4, 272], P('col', 'row', 'dp'), may hold values from -0.1875 to 0.1875
- qkv_bias: float32 [4, 816], P('col', 'dp'), may hold values from -1.5 to 1.5
- fc1_bias: float32 [4, 1088], P('col', 'dp'), may hold values from -1.75 to 1.75
- row_vectors: float32 [6, 4, 272], P(None, 'row', 'dp'), may hold values from -1.5 to 1.5, as said below
- qkv_moments: float32 [2, 1088, 4, 816], P(None, 'row', 'col', 'dp'), may hold values from -0.45 to 0.45, as said below
- proj_moments: float32 [2, 1088, 4, 272], P(None, 'col', 'row', 'dp'), may hold values from -0.075 to 0.075, as said below
- fc1_moments: float32 [2, 1088, 4, 1088], P(None, 'row', 'col', 'dp'), may hold values from -0.105 to 0.105, as said below
- fc2_moments: float32 [2, 4352, 4, 272], P(None, 'col', 'row', 'dp'), may hold values from -0.18 to 0.18, as said below
- qkv_bias_moments: float32 [2, 4, 816], P(None, 'col', 'dp'), may hold values from -0.75 to 0.75, as said below
- fc1_bias_moments: float32 [2, 4, 1088], P(None, 'col', 'dp'), may hold values from -0.105 to 0.105, as said below
- row_moments: float32 [2, 6, 4, 272], P(None, None, 'row', 'dp'), may hold values from -0.6 to 0.6, as said below
Outputs:
- block_out: bfloat16 [4096, 1088], P(('dp', 'col'), 'row')
- block_in_grad: float32 [4096, 1088], P(('dp', 'col'), 'row')
- qkv_weight_grad: float32 [1088, 4, 816], P('row', 'col', 'dp')
- proj_weight_grad: float32 [1088, 4, 272], P('col', 'row', 'dp')
- fc1_weight_grad: float32 [1088, 4, 1088], P('row', 'col', 'dp')
- fc2_weight_grad: float32 [4352, 4, 272], P('col', 'row', 'dp')
- qkv_bias_grad: float32 [4, 816], P('col', 'dp')
- fc1_bias_grad: float32 [4, 1088], P('col', 'dp')
- row_vectors_grad: float32 [6, 4, 272], P(None, 'row', 'dp')
- qkv_weight_new: float32 [1088, 4, 816], P('row', 'col', 'dp')
- proj_weight_new: float32 [1088, 4, 272], P('col', 'row', 'dp')
- fc1_weight_new: float32 [1088, 4, 1088], P('row', 'col', 'dp')
- fc2_weight_new: float32 [4352, 4, 272], P('col', 'row', 'dp')
- qkv_bias_new: float32 [4, 816], P('col', 'dp')
- fc1_bias_new: float32 [4, 1088], P('col', 'dp')
- row_vectors_new: float32 [6, 4, 272], P(None, 'row', 'dp')
- qkv_moments_new: float32 [2, 1088, 4, 816], P(None, 'row', 'col', 'dp')
- proj_moments_new: float32 [2, 1088, 4, 272], P(None, 'col', 'row', 'dp')
- fc1_moments_new: float32 [2, 1088, 4, 1088], P(None, 'row', 'col', 'dp')
- fc2_moments_new: float32 [2, 4352, 4, 272], P(None, 'col', 'row', 'dp')
- qkv_bias_moments_new: float32 [2, 4, 816], P(None, 'col', 'dp')
- fc1_bias_moments_new: float32 [2, 4, 1088], P(None, 'col', 'dp')
- row_moments_new: float32 [2, 6, 4, 272], P(None, None, 'row', 'dp')
The draws below stay inside these ranges and needn't reach their ends.
Inputs may be any that keep to these rules, and one draw needn't show every extreme that they name: In every row the 3 lengths sum to 512 and one of them equals 384. `row_vectors`: rows 0 and 3 are gains, the other rows biases. `qkv_moments`: index 0 holds first moments, index 1 second moments, which are positive. `proj_moments`: index 0 holds first moments, index 1 second moments, which are positive. `fc1_moments`: index 0 holds first moments, index 1 second moments, which are positive. `fc2_moments`: index 0 holds first moments, index 1 second moments, which are positive. `qkv_bias_moments`: index 0 holds first moments, index 1 second moments, which are positive. `fc1_bias_moments`: index 0 holds first moments, index 1 second moments, which are positive. `row_moments`: index 0 holds first moments, index 1 second moments, which are positive.
All inputs are finite; a program needn't handle non-finite values.
Results may differ from the reference program's by a relative error of at most 0.018.
Values may be sent and summed in bfloat16 or wider, within the bound.
A program may use at most 128 MiB of HBM per device.

```python
import math
import jax
import jax.numpy as jnp
import numpy as np
from jax import lax

D = 1088
H = 17
HD = 64
FF = 4352
PACK = 512
SEQS = 3
STEP = 3
MAXLEN = 384
GROUP = 2048
TOKENS = 4096
PACKS = 8
N_DP = 2
N_ROW = 4
N_COL = 4


def moment_pair(key, shape, typical):
    first_moment = jnp.clip(0.1 * typical * jax.random.normal(jax.random.fold_in(key, 11), shape, jnp.float32), -0.3 * typical, 0.3 * typical)
    second_moment = typical * typical * jnp.exp(jax.random.uniform(jax.random.fold_in(key, 12), shape, jnp.float32, math.log(0.01), math.log(0.1)))
    return jnp.stack([first_moment, second_moment])


def draw_qkv_moments(key, part):
    return moment_pair(key, (D, N_COL, 3 * D // N_COL), 1.5)


def draw_proj_moments(key, part):
    return moment_pair(key, (D, N_ROW, D // N_ROW), 0.25)


def draw_fc1_moments(key, part):
    return moment_pair(key, (D, N_COL, FF // N_COL), 0.35)


def draw_fc2_moments(key, part):
    return moment_pair(key, (FF, N_ROW, D // N_ROW), 0.6)


def draw_qkv_bias_moments(key, part):
    return moment_pair(key, (N_COL, 3 * D // N_COL), 2.5)


def draw_fc1_bias_moments(key, part):
    return moment_pair(key, (N_COL, FF // N_COL), 0.35)


def draw_row_moments(key, part):
    return moment_pair(key, (6, N_ROW, D // N_ROW), 2.0)


def draw_row_vectors(key, part):
    gain_draw = jax.random.uniform(jax.random.fold_in(key, 21), (6, D), jnp.float32, 0.5, 1.5)
    bias_draw = jnp.clip(0.3 * jax.random.normal(jax.random.fold_in(key, 22), (6, D), jnp.float32), -1.5, 1.5)
    is_gain = (jnp.arange(6) % 3 == 0)[:, None]
    return jnp.where(is_gain, gain_draw, bias_draw).reshape(6, N_ROW, D // N_ROW)


def draw_qkv_bias(key, part):
    base_draw = jnp.clip(0.3 * jax.random.normal(jax.random.fold_in(key, 31), (3 * D,), jnp.float32), -1.5, 1.5)
    return base_draw.reshape(N_COL, 3 * D // N_COL)


def shard_levels(stream_key, dims, pieces, smallest, top_value):
    def one(position, parts):
        heights = jax.random.uniform(jax.random.fold_in(jax.random.fold_in(stream_key, 6), position), (parts,), jnp.float32, smallest / len(pieces), top_value / len(pieces))
        return jnp.repeat(jnp.exp(heights), dims[position] // parts).reshape((-1,) + (1,) * (len(dims) - position - 1))

    gain = one(*pieces[0])
    for cut in pieces[1:]:
        gain = gain * one(*cut)
    return gain


def split_up(number_of, total, reach, skew):
    weights = [(1 << 20) // math.isqrt(standing ** skew) + 1 for standing in range(2, number_of + 1)]
    spare, counts = total - reach - (number_of - 1), [1] * (number_of - 1)
    while spare > 0:
        movable = [i for i in range(number_of - 1) if counts[i] < reach]
        pool, left = sum([weights[i] for i in movable]), spare
        for i in movable:
            more = min(reach - counts[i], max(1, left * weights[i] // pool), spare)
            counts[i] = counts[i] + more
            spare = spare - more
    return np.array([reach] + counts)


def ragged(own_key, count, total, most, lean):
    if count == 2:
        one = jax.random.randint(own_key, (), max(1, total - most), min(most, total - 1) + 1)
        return jnp.stack([one, total - one])
    sizes = jnp.asarray(split_up(count, total, most, lean), jnp.int32)
    pairs = (count - 1) // 2
    donor, sink = sizes[1:1 + 2 * pairs:2], sizes[2:2 + 2 * pairs:2]
    room = jnp.minimum(donor - 1, most - sink)
    shifted = jax.random.randint(jax.random.fold_in(own_key, 1), (pairs,), 0, 1 << 20) % (room + 1)
    sizes = sizes.at[1:1 + 2 * pairs:2].set(donor - shifted).at[2:2 + 2 * pairs:2].set(sink + shifted)
    return sizes[jax.random.permutation(jax.random.fold_in(own_key, 2), count)]


def noise(stream_key, extent, deviation, reach, split=(), dtype=jnp.bfloat16):
    array = jax.random.normal(stream_key, extent, jnp.float32) * deviation
    if len(split) > 0:
        array = shard_levels(stream_key, extent, split, -0.22, 0.18) * array
    return jnp.clip(array, min=-reach, max=reach).astype(dtype)


def setup_inputs(seed: int = 0) -> dict:
    keys = jax.random.split(jax.random.key(seed), 18)
    block_in = noise(keys[0], (TOKENS, D), 1.0, 6.0, ((0, 8), (1, 4)))
    cotangent = noise(keys[1], (TOKENS, D), 0.007, 0.0390625, ((0, 8), (1, 4)))
    lengths = jax.vmap(lambda own: ragged(own, SEQS, PACK, MAXLEN, 2))(jax.random.split(keys[2], PACKS)).reshape((PACKS, SEQS)).astype(jnp.int32)
    qkv_weight = noise(keys[3], (D, N_COL, 3 * D // N_COL), D ** -0.5, 0.1875, ((0, 4), (1, 4), (2, 2)), jnp.float32)
    proj_weight = noise(keys[4], (D, N_ROW, D // N_ROW), (D // 64) ** -0.5, 1.5, ((0, 4), (1, 4), (2, 2)), jnp.float32)
    fc1_weight = noise(keys[5], (D, N_COL, FF // N_COL), (D // 2) ** -0.5, 0.25, ((0, 4), (1, 4), (2, 2)), jnp.float32)
    fc2_weight = noise(keys[6], (FF, N_ROW, D // N_ROW), (FF // 4) ** -0.5, 0.1875, ((0, 4), (1, 4), (2, 2)), jnp.float32)
    qkv_bias = draw_qkv_bias(jax.random.fold_in(keys[17], 71), 0)
    fc1_bias = noise(keys[8], (N_COL, FF // N_COL), 0.3, 1.75, ((0, 4), (1, 2)), jnp.float32)
    row_vectors = draw_row_vectors(jax.random.fold_in(keys[17], 71), 0)
    qkv_moments = draw_qkv_moments(jax.random.fold_in(keys[17], 71), 0)
    proj_moments = draw_proj_moments(jax.random.fold_in(keys[17], 71), 0)
    fc1_moments = draw_fc1_moments(jax.random.fold_in(keys[17], 71), 0)
    fc2_moments = draw_fc2_moments(jax.random.fold_in(keys[17], 71), 0)
    qkv_bias_moments = draw_qkv_bias_moments(jax.random.fold_in(keys[17], 71), 0)
    fc1_bias_moments = draw_fc1_bias_moments(jax.random.fold_in(keys[17], 71), 0)
    row_moments = draw_row_moments(jax.random.fold_in(keys[17], 71), 0)
    return dict(block_in=block_in, cotangent=cotangent, lengths=lengths, qkv_weight=qkv_weight, proj_weight=proj_weight, fc1_weight=fc1_weight, fc2_weight=fc2_weight, qkv_bias=qkv_bias, fc1_bias=fc1_bias, row_vectors=row_vectors, qkv_moments=qkv_moments, proj_moments=proj_moments, fc1_moments=fc1_moments, fc2_moments=fc2_moments, qkv_bias_moments=qkv_bias_moments, fc1_bias_moments=fc1_bias_moments, row_moments=row_moments)


NORM_EPS = 1e-05
BETA_ONE = 0.9
BETA_TWO = 0.95
LEARN_RATE = 0.05
VECTOR_RATE = 0.2
DECAY_RATE = 0.1
ADAM_EPS = 1e-08

def gelu_tanh(values_in):
    return jax.nn.gelu(values_in, approximate=True)

def rounded(values_in):
    return lax.optimization_barrier(values_in.astype(jnp.bfloat16)).astype(jnp.float32)

def norm_forward(values_in, gain_row, shift_row):
    row_mean = lax.optimization_barrier(jnp.mean(values_in, axis=1, keepdims=True))
    spread = lax.optimization_barrier(jnp.mean(values_in * values_in, axis=1, keepdims=True)) - row_mean * row_mean
    inv_scale = lax.rsqrt(spread + NORM_EPS)
    centred = (values_in - row_mean) * inv_scale
    return ((centred * gain_row + shift_row).astype(jnp.bfloat16), centred, inv_scale)

def norm_backward(upstream, centred, inv_scale, gain_row):
    pushed = upstream * gain_row
    result = inv_scale * (pushed - lax.optimization_barrier(jnp.mean(pushed, axis=1, keepdims=True)) - centred * lax.optimization_barrier(jnp.mean(pushed * centred, axis=1, keepdims=True)))
    return (result, lax.optimization_barrier(jnp.sum(upstream * centred, axis=0)), lax.optimization_barrier(jnp.sum(upstream, axis=0)))

def pack_mask(pack_lengths):
    seq_ends = jnp.cumsum(pack_lengths)
    places = jnp.arange(PACK)
    segment = lax.optimization_barrier(jnp.sum((places[:, None] >= seq_ends[None, :]).astype(jnp.int32), axis=1))
    return (segment[:, None] == segment[None, :]) & (places[None, :] <= places[:, None])

def split_heads(packed):
    queries = packed[:, :D].reshape(PACK, H, HD)
    key_heads = packed[:, D:2 * D].reshape(PACK, H, HD)
    value_heads = packed[:, 2 * D:].reshape(PACK, H, HD)
    return (queries, key_heads, value_heads)

def attention_scores(queries, key_heads, allowed):
    scores = jnp.einsum('qhd,khd->hqk', queries.astype(jnp.float32), key_heads.astype(jnp.float32)) * HD ** (-0.5)
    return jnp.where(allowed[None], scores, -1e+30)

def attention_forward(packed, allowed):
    queries, key_heads, value_heads = split_heads(packed)
    scores = attention_scores(queries, key_heads, allowed)
    row_top = lax.optimization_barrier(jnp.max(scores, axis=2, keepdims=True))
    log_total = row_top + jnp.log(lax.optimization_barrier(jnp.sum(jnp.exp(scores - row_top), axis=2, keepdims=True)))
    weights = rounded(jnp.exp(scores - log_total))
    attended = jnp.einsum('hqk,khd->qhd', weights, value_heads.astype(jnp.float32)).astype(jnp.bfloat16)
    return (attended.reshape(PACK, D), log_total)

def attention_backward(packed, allowed, attended, log_total, grad_att):
    queries, key_heads, value_heads = split_heads(packed)
    scores = attention_scores(queries, key_heads, allowed)
    probs_full = jnp.exp(scores - log_total)
    probs_short = rounded(probs_full)
    grad_heads = grad_att.reshape(PACK, H, HD).astype(jnp.float32)
    grad_values = jnp.einsum('hqk,qhd->khd', probs_short, grad_heads)
    grad_probs = jnp.einsum('qhd,khd->hqk', grad_heads, value_heads.astype(jnp.float32))
    row_delta = lax.optimization_barrier(jnp.sum(grad_heads * attended.reshape(PACK, H, HD).astype(jnp.float32), axis=2))
    grad_scores = rounded(probs_full * (grad_probs - row_delta.T[:, :, None]) * HD ** (-0.5))
    grad_query = jnp.einsum('hqk,khd->qhd', grad_scores, key_heads.astype(jnp.float32))
    grad_keys = jnp.einsum('hqk,qhd->khd', grad_scores, queries.astype(jnp.float32))
    return jnp.concatenate([grad_query.reshape(PACK, D), grad_keys.reshape(PACK, D), grad_values.reshape(PACK, D)], axis=1)

def adam_step(master, moment, gradient, decay_rate, step_rate):
    first_moment = BETA_ONE * moment[0] + (1.0 - BETA_ONE) * gradient
    second_moment = BETA_TWO * moment[1] + (1.0 - BETA_TWO) * gradient * gradient
    change = first_moment / (1.0 - BETA_ONE ** STEP) / (jnp.sqrt(second_moment / (1.0 - BETA_TWO ** STEP)) + ADAM_EPS)
    change = change + decay_rate * master
    return (master - step_rate * change, jnp.stack([first_moment, second_moment]))

def reference(block_in, cotangent, lengths, qkv_weight, proj_weight, fc1_weight, fc2_weight, qkv_bias, fc1_bias, row_vectors, qkv_moments, proj_moments, fc1_moments, fc2_moments, qkv_bias_moments, fc1_bias_moments, row_moments):
    wide_type = jnp.float32
    short_type = jnp.bfloat16
    w_qkv = lax.optimization_barrier(qkv_weight.astype(short_type)).reshape(D, 3 * D)
    w_proj = lax.optimization_barrier(proj_weight.astype(short_type)).reshape(D, D)
    w_fc1 = lax.optimization_barrier(fc1_weight.astype(short_type)).reshape(D, FF)
    w_fc2 = lax.optimization_barrier(fc2_weight.astype(short_type)).reshape(FF, D)
    bias_qkv = rounded(qkv_bias).reshape(3 * D)
    bias_fc1 = rounded(fc1_bias).reshape(FF)
    vectors = rounded(row_vectors).reshape(6, D)

    def one_group(totals, group):
        x_in, grad_out, group_lengths = group
        x_full = x_in.astype(wide_type)
        normed_one, centred_one, scale_one = norm_forward(x_full, vectors[0], vectors[1])
        mixed_qkv = (jnp.dot(normed_one, w_qkv, preferred_element_type=wide_type) + bias_qkv).astype(short_type)
        packed = mixed_qkv.reshape(N_ROW, PACK, 3 * D)
        allowed = jax.vmap(pack_mask)(group_lengths)
        attended, log_total = jax.vmap(attention_forward)(packed, allowed)
        heads_all = attended.reshape(GROUP, D)
        x_mid = x_full + jnp.dot(heads_all, w_proj, preferred_element_type=wide_type) + vectors[2]
        normed_two, centred_two, scale_two = norm_forward(x_mid, vectors[3], vectors[4])
        pre_act = jnp.dot(normed_two, w_fc1, preferred_element_type=wide_type) + bias_fc1
        hidden = gelu_tanh(pre_act).astype(short_type)
        block_out = (x_mid + jnp.dot(hidden, w_fc2, preferred_element_type=wide_type) + vectors[5]).astype(short_type)
        grad_fc2 = jnp.dot(hidden.T, grad_out, preferred_element_type=wide_type)
        grad_bias_two = lax.optimization_barrier(jnp.sum(grad_out.astype(wide_type), axis=0))
        grad_hidden = jnp.dot(grad_out, w_fc2.T, preferred_element_type=wide_type)
        pullback = jax.vjp(gelu_tanh, pre_act)[1]
        grad_pre = pullback(grad_hidden)[0].astype(short_type)
        grad_fc1 = jnp.dot(normed_two.T, grad_pre, preferred_element_type=wide_type)
        grad_bias_fc1 = lax.optimization_barrier(jnp.sum(grad_pre.astype(wide_type), axis=0))
        grad_normed_two = jnp.dot(grad_pre, w_fc1.T, preferred_element_type=wide_type)
        back_two, grad_gain_two, grad_shift_two = norm_backward(grad_normed_two, centred_two, scale_two, vectors[3])
        grad_mid = grad_out.astype(wide_type) + back_two
        grad_mid_short = grad_mid.astype(short_type)
        grad_proj = jnp.dot(heads_all.T, grad_mid_short, preferred_element_type=wide_type)
        grad_bias_proj = lax.optimization_barrier(jnp.sum(grad_mid_short.astype(wide_type), axis=0))
        grad_heads = jnp.dot(grad_mid_short, w_proj.T, preferred_element_type=wide_type).astype(short_type)
        grad_packs = jax.vmap(attention_backward)(packed, allowed, attended, log_total, grad_heads.reshape(N_ROW, PACK, D))
        grad_mixed = grad_packs.reshape(GROUP, 3 * D).astype(short_type)
        grad_qkv = jnp.dot(normed_one.T, grad_mixed, preferred_element_type=wide_type)
        grad_bias_qkv = lax.optimization_barrier(jnp.sum(grad_mixed.astype(wide_type), axis=0))
        grad_normed_one = jnp.dot(grad_mixed, w_qkv.T, preferred_element_type=wide_type)
        back_one, grad_gain_one, grad_shift_one = norm_backward(grad_normed_one, centred_one, scale_one, vectors[0])
        grad_in = grad_mid + back_one
        row_grads = jnp.stack([grad_gain_one, grad_shift_one, grad_bias_proj, grad_gain_two, grad_shift_two, grad_bias_two])
        found = (grad_qkv, grad_proj, grad_fc1, grad_fc2, grad_bias_qkv, grad_bias_fc1, row_grads)
        totals = tuple((old + new for old, new in zip(totals, found)))
        return (totals, (block_out, grad_in))
    zero_grads = (jnp.zeros((D, 3 * D), wide_type), jnp.zeros((D, D), wide_type), jnp.zeros((D, FF), wide_type), jnp.zeros((FF, D), wide_type), jnp.zeros((3 * D,), wide_type), jnp.zeros((FF,), wide_type), jnp.zeros((6, D), wide_type))
    groups_in = (block_in.reshape(N_DP, GROUP, D), cotangent.reshape(N_DP, GROUP, D), lengths.reshape(N_DP, N_ROW, SEQS))
    totals, outs_seq = lax.scan(one_group, zero_grads, groups_in)
    block_out = outs_seq[0].reshape(TOKENS, D)
    block_in_grad = outs_seq[1].reshape(TOKENS, D)
    masters = (qkv_weight, proj_weight, fc1_weight, fc2_weight, qkv_bias, fc1_bias, row_vectors)
    moments = (qkv_moments, proj_moments, fc1_moments, fc2_moments, qkv_bias_moments, fc1_bias_moments, row_moments)
    decays = (DECAY_RATE, DECAY_RATE, DECAY_RATE, DECAY_RATE, 0.0, 0.0, 0.0)
    rates = (LEARN_RATE, LEARN_RATE, LEARN_RATE, LEARN_RATE, VECTOR_RATE, VECTOR_RATE, VECTOR_RATE)
    grads = tuple((total.reshape(master.shape) for total, master in zip(totals, masters)))
    updates = [adam_step(master, moment, gradient, decay_rate, step_rate) for master, moment, gradient, decay_rate, step_rate in zip(masters, moments, grads, decays, rates)]
    return (block_out, block_in_grad, grads[0], grads[1], grads[2], grads[3], grads[4], grads[5], grads[6], updates[0][0], updates[1][0], updates[2][0], updates[3][0], updates[4][0], updates[5][0], updates[6][0], updates[0][1], updates[1][1], updates[2][1], updates[3][1], updates[4][1], updates[5][1], updates[6][1])
```

```python
import jax
import jax.numpy as jnp
from jax import lax
from jax.sharding import PartitionSpec as P

D = 1088
H = 17
HD = 64
STEP = 3
EXT = 320
HALO = 48


NORM_EPS = 1e-05
BETA_ONE = 0.9
BETA_TWO = 0.95
LEARN_RATE = 0.05
VECTOR_RATE = 0.2
DECAY_RATE = 0.1
ADAM_EPS = 1e-08


def gelu_tanh(values_in):
    return jax.nn.gelu(values_in, approximate=True)


def weigh(row_block, weight, transposed):
    return lax.dot_general(
        row_block,
        weight,
        (((1,), (1 if transposed else 0,)), ((), ())),
        preferred_element_type=jnp.float32,
    )


def outer_sum(left_rows, right_rows):
    return lax.dot_general(
        left_rows, right_rows, (((0,), (0,)), ((), ())), preferred_element_type=jnp.float32
    )


def swap_grid(block):
    count = lax.axis_size("row")
    pairs = [(r * count + c, c * count + r) for r in range(count) for c in range(count)]
    return lax.ppermute(block, ("row", "col"), pairs)


def row_stats(values_in):
    row_mean = jnp.mean(values_in, axis=1, keepdims=True)
    spread = jnp.mean(values_in * values_in, axis=1, keepdims=True) - row_mean * row_mean
    return row_mean, lax.rsqrt(spread + NORM_EPS)


def norm_backward(upstream, centred, inv_scale, gain_row):
    pushed = upstream * gain_row
    row_total = jnp.mean(pushed, axis=1, keepdims=True)
    cross = jnp.mean(pushed * centred, axis=1, keepdims=True)
    result = inv_scale * (pushed - row_total - centred * cross)
    return (result, jnp.sum(upstream * centred, axis=0), jnp.sum(upstream, axis=0))


def reduce_rows(grad):
    return lax.psum_scatter(grad, "row", scatter_dimension=0, tiled=True)


def reduce_groups(grad, dim):
    count = lax.axis_size("dp")
    if count != 2:
        return lax.psum_scatter(grad, "dp", scatter_dimension=dim, tiled=True)
    half = grad.shape[dim] // 2
    mine = lax.axis_index("dp")
    kept = lax.dynamic_slice_in_dim(grad, mine * half, half, dim)
    sent = lax.dynamic_slice_in_dim(grad, (1 - mine) * half, half, dim)
    return kept.astype(jnp.float32) + lax.ppermute(sent, "dp", [(0, 1), (1, 0)]).astype(jnp.float32)


def split_heads(columns):
    rows = columns.shape[0]
    return columns.reshape(rows, EXT // HD, HD).transpose(1, 0, 2)


def join_heads(heads):
    return heads.transpose(1, 0, 2).reshape(heads.shape[1], EXT)


def batched(spec, left, right):
    return jnp.einsum(spec, left, right, preferred_element_type=jnp.float32)


def adam_step(master, moment, gradient, decay_rate, step_rate):
    first_moment = BETA_ONE * moment[0] + (1.0 - BETA_ONE) * gradient
    second_moment = BETA_TWO * moment[1] + (1.0 - BETA_TWO) * gradient * gradient
    change = (
        first_moment
        / (1.0 - BETA_ONE**STEP)
        / (jnp.sqrt(second_moment / (1.0 - BETA_TWO**STEP)) + ADAM_EPS)
    )
    change = change + decay_rate * master
    return (master - step_rate * change, jnp.stack([first_moment, second_moment]))


def on_device(
    block_in,
    cotangent,
    lengths,
    qkv_weight,
    proj_weight,
    fc1_weight,
    fc2_weight,
    qkv_bias,
    fc1_bias,
    row_vectors,
    qkv_moments,
    proj_moments,
    fc1_moments,
    fc2_moments,
    qkv_bias_moments,
    fc1_bias_moments,
    row_moments,
):
    wide = jnp.float32
    short = jnp.bfloat16
    my_col = lax.axis_index("col")
    my_row = lax.axis_index("row")
    my_dp = lax.axis_index("dp")
    n_dp = lax.axis_size("dp")
    n_col = lax.axis_size("col")
    n_row = lax.axis_size("row")
    part = D // n_col
    pack_len = block_in.shape[0]

    x_part = swap_grid(block_in)
    x_bf = lax.all_gather(x_part, "col", axis=1, tiled=True)
    cot_part = swap_grid(cotangent)
    cot = lax.all_gather(cot_part, "col", axis=1, tiled=True)

    small = jnp.concatenate(
        [row_vectors.reshape(-1), fc1_bias.reshape(-1), qkv_bias.reshape(-1)]
    ).astype(short)
    rv_size = row_vectors.size
    b1_size = fc1_bias.size
    small_all = lax.all_gather(small, ("row", "col", "dp"), axis=0, tiled=False)
    small_all = small_all.reshape(n_row, n_col, n_dp, small.shape[0]).astype(wide)
    vectors = (
        small_all[:, 0, :, :rv_size]
        .reshape(n_row, n_dp, 6, part // n_dp)
        .transpose(2, 0, 1, 3)
        .reshape(6, D)
    )
    bias_fc1 = lax.dynamic_index_in_dim(
        small_all[0, :, :, rv_size : rv_size + b1_size], my_col, 0, keepdims=False
    ).reshape(-1)
    bias_qkv_all = small_all[0, :, :, rv_size + b1_size :].reshape(3, D)

    ext_start = my_col * (EXT - HD)
    own_start = my_col * (part - (EXT - HD))
    qkv_cols = lax.all_gather(
        qkv_weight[:, 0, :].astype(short), ("col", "dp"), axis=1, tiled=True
    )
    qkv_ext = jnp.concatenate(
        [lax.dynamic_slice_in_dim(qkv_cols, i * D + ext_start, EXT, 1) for i in range(3)], axis=1
    )
    w_qkv = lax.all_gather(qkv_ext, "row", axis=0, tiled=True)
    bias_qkv = lax.dynamic_slice_in_dim(bias_qkv_all, ext_start, EXT, 1).reshape(-1)

    proj_t = proj_weight[:, 0, :].astype(short).T
    halo = HALO
    from_left = lax.ppermute(
        proj_t[:, part - halo :], "col", [(i, i + 1) for i in range(n_col - 1)]
    )
    from_right = lax.ppermute(proj_t[:, :halo], "col", [(i + 1, i) for i in range(n_col - 1)])
    proj_ext = lax.dynamic_slice_in_dim(
        jnp.concatenate([from_left, proj_t, from_right], axis=1), halo - own_start, EXT, 1
    )
    w_proj_t = lax.all_gather(proj_ext, ("row", "dp"), axis=0, tiled=True)
    fc1_cols = lax.all_gather(fc1_weight[:, 0, :].astype(short), "dp", axis=1, tiled=True)
    w_fc1 = lax.all_gather(fc1_cols, "row", axis=0, tiled=True)
    w_fc2_t = lax.all_gather(
        fc2_weight[:, 0, :].astype(short).T, ("row", "dp"), axis=0, tiled=True
    )

    x_full = x_bf.astype(wide)
    mean_one, scale_one = row_stats(x_full)
    centred_one = (x_full - mean_one) * scale_one
    normed_one = (centred_one * vectors[0] + vectors[1]).astype(short)
    mixed = (weigh(normed_one, w_qkv, False) + bias_qkv).astype(short)
    queries = split_heads(mixed[:, :EXT])
    keys = split_heads(mixed[:, EXT : 2 * EXT])
    values = split_heads(mixed[:, 2 * EXT :])
    seq_ends = jnp.cumsum(lengths[0])
    places = jnp.arange(pack_len, dtype=jnp.int32)
    segment = jnp.sum((places[:, None] >= seq_ends[None, :]).astype(jnp.int32), axis=1)
    allowed = (segment[:, None] == segment[None, :]) & (places[None, :] <= places[:, None])
    scores = jnp.where(
        allowed[None], batched("hqd,hkd->hqk", queries, keys) * HD ** (-0.5), -1e30
    )
    row_top = jnp.max(scores, axis=2, keepdims=True)
    log_total = row_top + jnp.log(jnp.sum(jnp.exp(scores - row_top), axis=2, keepdims=True))
    probs = jnp.exp(scores - log_total)
    weights = probs.astype(short)
    attended = batched("hqk,hkd->hqd", weights, values).astype(short)
    own = jnp.arange(EXT)
    own = (own >= own_start) & (own < own_start + part)
    att_own = jnp.where(own[None, :], join_heads(attended), 0).astype(short)
    x_mid = (
        x_full
        + lax.psum(weigh(att_own, w_proj_t, True).astype(short), "col").astype(wide)
        + vectors[2]
    )

    mean_two, scale_two = row_stats(x_mid)
    centred_two = (x_mid - mean_two) * scale_two
    normed_two = (centred_two * vectors[3] + vectors[4]).astype(short)
    pre_act = weigh(normed_two, w_fc1, False) + bias_fc1
    hidden = gelu_tanh(pre_act).astype(short)
    out_part = lax.psum_scatter(
        weigh(hidden, w_fc2_t, True).astype(short), "col", scatter_dimension=1, tiled=True
    ).astype(wide)
    mid_part = lax.dynamic_slice_in_dim(x_mid, my_col * part, part, 1)
    shift_part = lax.dynamic_slice_in_dim(vectors[5], my_col * part, part, 0)
    block_out = swap_grid((mid_part + out_part + shift_part).astype(short))

    grad_hidden = weigh(cot, w_fc2_t, False)
    grad_pre = jax.vjp(gelu_tanh, pre_act)[1](grad_hidden)[0].astype(short)
    grad_fc2_t = outer_sum(cot, hidden).astype(short)
    shard_fc2 = reduce_groups(reduce_rows(grad_fc2_t), 0)
    grad_fc1 = outer_sum(normed_two, grad_pre).astype(short)
    shard_fc1 = reduce_groups(reduce_rows(grad_fc1), 1)
    cot_wide = cot.astype(wide)
    grad_bias_two = jnp.sum(cot_wide, axis=0)
    grad_bias_fc1 = jnp.sum(grad_pre.astype(wide), axis=0)
    grad_normed_two = lax.psum(weigh(grad_pre, w_fc1, True).astype(short), "col").astype(wide)
    back_two, gain_two, shift_two = norm_backward(
        grad_normed_two, centred_two, scale_two, vectors[3]
    )
    grad_mid = cot_wide + back_two
    grad_mid_short = grad_mid.astype(short)
    grad_bias_proj = jnp.sum(grad_mid_short.astype(wide), axis=0)
    grad_proj_t = lax.dynamic_slice_in_dim(
        outer_sum(grad_mid_short, att_own).astype(short), own_start, part, 1
    )
    shard_proj = reduce_groups(reduce_rows(grad_proj_t), 0)
    grad_att = split_heads(weigh(grad_mid_short, w_proj_t, False).astype(short))
    grad_values = batched("hqk,hqd->hkd", weights, grad_att)
    grad_probs = batched("hqd,hkd->hqk", grad_att, values)
    delta = jnp.sum(grad_att.astype(wide) * attended.astype(wide), axis=2, keepdims=True)
    grad_scores = (probs * (grad_probs - delta) * HD ** (-0.5)).astype(short)
    grad_query = batched("hqk,hkd->hqd", grad_scores, keys)
    grad_keys = batched("hqk,hqd->hkd", grad_scores, queries)
    units = [
        lax.dynamic_slice_in_dim(join_heads(grad.astype(short)), own_start, part, 1)
        for grad in (grad_query, grad_keys, grad_values)
    ]
    grad_ext = jnp.concatenate(
        [
            jnp.where(own[None, :], join_heads(grad.astype(short)), 0).astype(short)
            for grad in (grad_query, grad_keys, grad_values)
        ],
        axis=1,
    )
    stacked = jnp.stack(units)
    picks = [
        lax.dynamic_index_in_dim(stacked, jnp.array(table)[my_col], 0, keepdims=False)
        for table in ((0, 1, 1, 2), (1, 0, 2, 1), (2, 2, 0, 0))
    ]
    unit_b = lax.ppermute(picks[1], "col", [(0, 1), (1, 0), (2, 3), (3, 2)])
    unit_c = lax.ppermute(picks[2], "col", [(0, 2), (2, 0), (1, 3), (3, 1)])
    odd = (my_col % 2) == 1
    grad_block = jnp.concatenate(
        [jnp.where(odd, unit_c, picks[0]), unit_b, jnp.where(odd, picks[0], unit_c)], axis=1
    )
    grad_normed_one = lax.psum(weigh(grad_ext, w_qkv, True).astype(short), "col").astype(wide)
    grad_qkv = outer_sum(normed_one, grad_block).astype(short)
    shard_qkv = reduce_groups(reduce_rows(grad_qkv), 1)
    grad_bias_qkv = jnp.sum(grad_block.astype(wide), axis=0)
    back_one, gain_one, shift_one = norm_backward(
        grad_normed_one, centred_one, scale_one, vectors[0]
    )
    in_grad = lax.dynamic_slice_in_dim(grad_mid + back_one, my_col * part, part, 1)
    block_in_grad = swap_grid(in_grad.astype(short)).astype(wide)

    row_grads = jnp.stack(
        [gain_one, shift_one, grad_bias_proj, gain_two, shift_two, grad_bias_two]
    )
    sums = lax.psum(
        jnp.concatenate([row_grads.reshape(-1), grad_bias_fc1, grad_bias_qkv]), ("row", "dp")
    )
    vec_size = part // n_dp
    row_shard = lax.dynamic_slice_in_dim(
        sums[: 6 * D].reshape(6, D), my_row * part + my_dp * vec_size, vec_size, 1
    )[:, None, :]
    fc1_bias_shard = lax.dynamic_slice_in_dim(
        sums[6 * D : 6 * D + grad_bias_fc1.shape[0]], my_dp * b1_size, b1_size, 0
    )[None, :]
    qkv_bias_shard = lax.dynamic_slice_in_dim(
        sums[6 * D + grad_bias_fc1.shape[0] :], my_dp * qkv_bias.size, qkv_bias.size, 0
    )[None, :]
    grads = (
        shard_qkv.astype(wide)[:, None, :],
        shard_proj.astype(wide).T[:, None, :],
        shard_fc1.astype(wide)[:, None, :],
        shard_fc2.astype(wide).T[:, None, :],
        qkv_bias_shard,
        fc1_bias_shard,
        row_shard,
    )
    masters = (qkv_weight, proj_weight, fc1_weight, fc2_weight, qkv_bias, fc1_bias, row_vectors)
    moments = (
        qkv_moments,
        proj_moments,
        fc1_moments,
        fc2_moments,
        qkv_bias_moments,
        fc1_bias_moments,
        row_moments,
    )
    decays = (DECAY_RATE, DECAY_RATE, DECAY_RATE, DECAY_RATE, 0.0, 0.0, 0.0)
    rates = (LEARN_RATE, LEARN_RATE, LEARN_RATE, LEARN_RATE, VECTOR_RATE, VECTOR_RATE, VECTOR_RATE)
    updates = [
        adam_step(master, moment, gradient, decay_rate, step_rate)
        for master, moment, gradient, decay_rate, step_rate in zip(
            masters, moments, grads, decays, rates
        )
    ]
    return (
        block_out,
        block_in_grad,
        grads[0],
        grads[1],
        grads[2],
        grads[3],
        grads[4],
        grads[5],
        grads[6],
        updates[0][0],
        updates[1][0],
        updates[2][0],
        updates[3][0],
        updates[4][0],
        updates[5][0],
        updates[6][0],
        updates[0][1],
        updates[1][1],
        updates[2][1],
        updates[3][1],
        updates[4][1],
        updates[5][1],
        updates[6][1],
    )


def solution(mesh):
    in_specs = (
        P(("dp", "col"), "row"),
        P(("dp", "col"), "row"),
        P(("dp", "row"), None),
        P("row", "col", "dp"),
        P("col", "row", "dp"),
        P("row", "col", "dp"),
        P("col", "row", "dp"),
        P("col", "dp"),
        P("col", "dp"),
        P(None, "row", "dp"),
        P(None, "row", "col", "dp"),
        P(None, "col", "row", "dp"),
        P(None, "row", "col", "dp"),
        P(None, "col", "row", "dp"),
        P(None, "col", "dp"),
        P(None, "col", "dp"),
        P(None, None, "row", "dp"),
    )
    out_specs = (
        P(("dp", "col"), "row"),
        P(("dp", "col"), "row"),
        P("row", "col", "dp"),
        P("col", "row", "dp"),
        P("row", "col", "dp"),
        P("col", "row", "dp"),
        P("col", "dp"),
        P("col", "dp"),
        P(None, "row", "dp"),
        P("row", "col", "dp"),
        P("col", "row", "dp"),
        P("row", "col", "dp"),
        P("col", "row", "dp"),
        P("col", "dp"),
        P("col", "dp"),
        P(None, "row", "dp"),
        P(None, "row", "col", "dp"),
        P(None, "col", "row", "dp"),
        P(None, "row", "col", "dp"),
        P(None, "col", "row", "dp"),
        P(None, "col", "dp"),
        P(None, "col", "dp"),
        P(None, None, "row", "dp"),
    )
    return jax.shard_map(
        on_device, mesh=mesh, in_specs=in_specs, out_specs=out_specs, check_vma=False
    )
```

```python
import jax
import jax.numpy as jnp
from jax import lax
from jax.sharding import PartitionSpec as P

D = 1088
H = 17
HD = 64
STEP = 3
EXT = 320
HALO = 48


NORM_EPS = 1e-05
BETA_ONE = 0.9
BETA_TWO = 0.95
LEARN_RATE = 0.05
VECTOR_RATE = 0.2
DECAY_RATE = 0.1
ADAM_EPS = 1e-08


def gelu_tanh(values_in):
    return jax.nn.gelu(values_in, approximate=True)


def weigh(row_block, weight, transposed):
    return lax.dot_general(
        row_block,
        weight,
        (((1,), (1 if transposed else 0,)), ((), ())),
        preferred_element_type=jnp.float32,
    )


def outer_sum(left_rows, right_rows):
    return lax.dot_general(
        left_rows, right_rows, (((0,), (0,)), ((), ())), preferred_element_type=jnp.float32
    )


def swap_grid(block):
    count = lax.axis_size("row")
    pairs = [(r * count + c, c * count + r) for r in range(count) for c in range(count)]
    return lax.ppermute(block, ("row", "col"), pairs)


def row_stats(values_in):
    row_mean = jnp.mean(values_in, axis=1, keepdims=True)
    spread = jnp.mean(values_in * values_in, axis=1, keepdims=True) - row_mean * row_mean
    return row_mean, lax.rsqrt(spread + NORM_EPS)


def norm_backward(upstream, centred, inv_scale, gain_row):
    pushed = upstream * gain_row
    row_total = jnp.mean(pushed, axis=1, keepdims=True)
    cross = jnp.mean(pushed * centred, axis=1, keepdims=True)
    result = inv_scale * (pushed - row_total - centred * cross)
    return (result, jnp.sum(upstream * centred, axis=0), jnp.sum(upstream, axis=0))


def step_right(block, senders):
    return lax.ppermute(block, "row", [(q, q + 1) for q in senders])


def step_left(block, senders):
    return lax.ppermute(block, "row", [(q, q - 1) for q in senders])


def gather_rows(block):
    count = lax.axis_size("row")
    mine = lax.axis_index("row")
    size = block.shape[0]
    from_left, from_right = [], []
    lefts, rights = block, block
    for step in range(1, count):
        lefts = step_right(lefts, range(step - 1, count - 1))
        rights = step_left(rights, range(1, count - step + 1))
        from_left.append(lefts)
        from_right.append(rights)
    whole = jnp.zeros((size * count,) + block.shape[1:], block.dtype)
    whole = lax.dynamic_update_slice_in_dim(whole, block, mine * size, 0)
    for step in range(1, count):
        piece = jnp.where(mine >= step, from_left[step - 1], from_right[count - step - 1])
        place = lax.rem(mine - step + count, count)
        whole = lax.dynamic_update_slice_in_dim(whole, piece, place * size, 0)
    return whole


def reduce_rows(grad):
    count = lax.axis_size("row")
    mine = lax.axis_index("row")
    size = grad.shape[0] // count

    def own_block(index):
        return lax.dynamic_slice_in_dim(grad, jnp.clip(index, 0, count - 1) * size, size, 0)

    lefts, rights = None, None
    for step in range(1, count):
        up = own_block(mine + count - step)
        down = own_block(mine - count + step)
        if lefts is not None:
            up = (up.astype(jnp.float32) + lefts.astype(jnp.float32)).astype(grad.dtype)
            down = (down.astype(jnp.float32) + rights.astype(jnp.float32)).astype(grad.dtype)
        lefts = step_right(up, range(step))
        rights = step_left(down, range(count - step, count))
    total = own_block(mine).astype(jnp.float32) + lefts.astype(jnp.float32)
    return (total + rights.astype(jnp.float32)).astype(grad.dtype)


def swap_cols(block, bit):
    return lax.ppermute(block, "col", [(c, c ^ bit) for c in range(lax.axis_size("col"))])


def gather_features(block):
    mine = lax.axis_index("col")
    near = swap_cols(block, 1)
    pair = jnp.stack([block, near])
    both = jnp.concatenate([pair, swap_cols(pair, 2)], axis=0)
    return jnp.concatenate(
        [
            lax.dynamic_index_in_dim(both, mine ^ j, 0, keepdims=False)
            for j in range(lax.axis_size("col"))
        ],
        axis=1,
    )


def sum_cols(part):
    half = part.shape[0] // 2
    side = lax.axis_index("col") % 2
    wide = jnp.float32
    kept = lax.dynamic_slice_in_dim(part, side * half, half, 0)
    sent = lax.dynamic_slice_in_dim(part, (1 - side) * half, half, 0)
    chip = (kept.astype(wide) + swap_cols(sent, 1).astype(wide)).astype(part.dtype)
    both = (chip.astype(wide) + swap_cols(chip, 2).astype(wide)).astype(part.dtype)
    other = swap_cols(both, 1)
    return jnp.where(
        side == 0,
        jnp.concatenate([both, other], axis=0),
        jnp.concatenate([other, both], axis=0),
    )


def gather_groups(block, dim):
    count = lax.axis_size("dp")
    if count != 2:
        return lax.all_gather(block, "dp", axis=dim, tiled=True)
    other = lax.ppermute(block, "dp", [(0, 1), (1, 0)])
    first = lax.axis_index("dp") == 0
    return jnp.where(
        first,
        jnp.concatenate([block, other], axis=dim),
        jnp.concatenate([other, block], axis=dim),
    )


def with_halo(units, own_start):
    count = lax.axis_size("col")
    width = units.shape[-1]
    from_left = lax.ppermute(
        units[..., width - HALO :], "col", [(i, i + 1) for i in range(count - 1)]
    )
    from_right = lax.ppermute(units[..., :HALO], "col", [(i + 1, i) for i in range(count - 1)])
    return lax.dynamic_slice_in_dim(
        jnp.concatenate([from_left, units, from_right], axis=-1),
        HALO - own_start,
        EXT,
        units.ndim - 1,
    )


def reduce_groups(grad, dim):
    count = lax.axis_size("dp")
    if count != 2:
        return lax.psum_scatter(grad, "dp", scatter_dimension=dim, tiled=True)
    half = grad.shape[dim] // 2
    mine = lax.axis_index("dp")
    kept = lax.dynamic_slice_in_dim(grad, mine * half, half, dim)
    sent = lax.dynamic_slice_in_dim(grad, (1 - mine) * half, half, dim)
    return kept.astype(jnp.float32) + lax.ppermute(sent, "dp", [(0, 1), (1, 0)]).astype(jnp.float32)


def split_heads(columns):
    rows = columns.shape[0]
    return columns.reshape(rows, EXT // HD, HD).transpose(1, 0, 2)


def join_heads(heads):
    return heads.transpose(1, 0, 2).reshape(heads.shape[1], EXT)


def batched(spec, left, right):
    return jnp.einsum(spec, left, right, preferred_element_type=jnp.float32)


def adam_step(master, moment, gradient, decay_rate, step_rate):
    first_moment = BETA_ONE * moment[0] + (1.0 - BETA_ONE) * gradient
    second_moment = BETA_TWO * moment[1] + (1.0 - BETA_TWO) * gradient * gradient
    change = (
        first_moment
        / (1.0 - BETA_ONE**STEP)
        / (jnp.sqrt(second_moment / (1.0 - BETA_TWO**STEP)) + ADAM_EPS)
    )
    change = change + decay_rate * master
    return (master - step_rate * change, jnp.stack([first_moment, second_moment]))


def on_device(
    block_in,
    cotangent,
    lengths,
    qkv_weight,
    proj_weight,
    fc1_weight,
    fc2_weight,
    qkv_bias,
    fc1_bias,
    row_vectors,
    qkv_moments,
    proj_moments,
    fc1_moments,
    fc2_moments,
    qkv_bias_moments,
    fc1_bias_moments,
    row_moments,
):
    wide = jnp.float32
    short = jnp.bfloat16
    my_col = lax.axis_index("col")
    my_row = lax.axis_index("row")
    my_dp = lax.axis_index("dp")
    n_dp = lax.axis_size("dp")
    n_col = lax.axis_size("col")
    n_row = lax.axis_size("row")
    part = D // n_col
    pack_len = block_in.shape[0]

    x_part = swap_grid(block_in)
    x_bf = gather_features(x_part)
    cot_part = swap_grid(cotangent)
    cot = gather_features(cot_part)

    small = jnp.concatenate(
        [row_vectors.reshape(-1), fc1_bias.reshape(-1), qkv_bias.reshape(-1)]
    ).astype(short)
    rv_size = row_vectors.size
    b1_size = fc1_bias.size
    small_all = lax.all_gather(small, ("row", "col", "dp"), axis=0, tiled=False)
    small_all = small_all.reshape(n_row, n_col, n_dp, small.shape[0]).astype(wide)
    vectors = (
        small_all[:, 0, :, :rv_size]
        .reshape(n_row, n_dp, 6, part // n_dp)
        .transpose(2, 0, 1, 3)
        .reshape(6, D)
    )
    bias_fc1 = lax.dynamic_index_in_dim(
        small_all[0, :, :, rv_size : rv_size + b1_size], my_col, 0, keepdims=False
    ).reshape(-1)
    bias_qkv_all = small_all[0, :, :, rv_size + b1_size :].reshape(3, D)

    ext_start = my_col * (EXT - HD)
    own_start = my_col * (part - (EXT - HD))
    odd = (my_col % 2) == 1
    qkv_block = gather_groups(qkv_weight[:, 0, :].astype(short), 1)
    first_unit, unit_b, last_unit = (qkv_block[:, i * part : (i + 1) * part] for i in range(3))
    arrived = jnp.stack(
        [
            jnp.where(odd, last_unit, first_unit),
            swap_cols(unit_b, 1),
            swap_cols(jnp.where(odd, first_unit, last_unit), 2),
        ]
    )
    qkv_units = jnp.stack(
        [
            lax.dynamic_index_in_dim(arrived, jnp.array(table)[my_col], 0, keepdims=False)
            for table in ((0, 1, 2, 2), (1, 0, 0, 1), (2, 2, 1, 0))
        ]
    )
    qkv_ext = with_halo(qkv_units, own_start)
    w_qkv = gather_rows(jnp.concatenate([qkv_ext[0], qkv_ext[1], qkv_ext[2]], axis=1))
    bias_qkv = lax.dynamic_slice_in_dim(bias_qkv_all, ext_start, EXT, 1).reshape(-1)

    proj_t = proj_weight[:, 0, :].astype(short).T
    w_proj_t = gather_rows(gather_groups(with_halo(proj_t, own_start), 0))
    w_fc1 = gather_rows(gather_groups(fc1_weight[:, 0, :].astype(short), 1))
    w_fc2_t = gather_rows(gather_groups(fc2_weight[:, 0, :].astype(short).T, 0))

    x_full = x_bf.astype(wide)
    mean_one, scale_one = row_stats(x_full)
    centred_one = (x_full - mean_one) * scale_one
    normed_one = (centred_one * vectors[0] + vectors[1]).astype(short)
    mixed = (weigh(normed_one, w_qkv, False) + bias_qkv).astype(short)
    queries = split_heads(mixed[:, :EXT])
    keys = split_heads(mixed[:, EXT : 2 * EXT])
    values = split_heads(mixed[:, 2 * EXT :])
    seq_ends = jnp.cumsum(lengths[0])
    places = jnp.arange(pack_len, dtype=jnp.int32)
    segment = jnp.sum((places[:, None] >= seq_ends[None, :]).astype(jnp.int32), axis=1)
    allowed = (segment[:, None] == segment[None, :]) & (places[None, :] <= places[:, None])
    scores = jnp.where(
        allowed[None], batched("hqd,hkd->hqk", queries, keys) * HD ** (-0.5), -1e30
    )
    row_top = jnp.max(scores, axis=2, keepdims=True)
    log_total = row_top + jnp.log(jnp.sum(jnp.exp(scores - row_top), axis=2, keepdims=True))
    probs = jnp.exp(scores - log_total)
    weights = probs.astype(short)
    attended = batched("hqk,hkd->hqd", weights, values).astype(short)
    own = jnp.arange(EXT)
    own = (own >= own_start) & (own < own_start + part)
    att_own = jnp.where(own[None, :], join_heads(attended), 0).astype(short)
    x_mid = (
        x_full
        + sum_cols(weigh(att_own, w_proj_t, True).astype(short)).astype(wide)
        + vectors[2]
    )

    mean_two, scale_two = row_stats(x_mid)
    centred_two = (x_mid - mean_two) * scale_two
    normed_two = (centred_two * vectors[3] + vectors[4]).astype(short)
    pre_act = weigh(normed_two, w_fc1, False) + bias_fc1
    hidden = gelu_tanh(pre_act).astype(short)
    out_part = lax.psum_scatter(
        weigh(hidden, w_fc2_t, True).astype(short), "col", scatter_dimension=1, tiled=True
    ).astype(wide)
    mid_part = lax.dynamic_slice_in_dim(x_mid, my_col * part, part, 1)
    shift_part = lax.dynamic_slice_in_dim(vectors[5], my_col * part, part, 0)
    block_out = swap_grid((mid_part + out_part + shift_part).astype(short))

    grad_hidden = weigh(cot, w_fc2_t, False)
    grad_pre = jax.vjp(gelu_tanh, pre_act)[1](grad_hidden)[0].astype(short)
    grad_fc2_t = outer_sum(cot, hidden).astype(short)
    shard_fc2 = reduce_groups(reduce_rows(grad_fc2_t), 0)
    grad_fc1 = outer_sum(normed_two, grad_pre).astype(short)
    shard_fc1 = reduce_groups(reduce_rows(grad_fc1), 1)
    cot_wide = cot.astype(wide)
    grad_bias_two = jnp.sum(cot_wide, axis=0)
    grad_bias_fc1 = jnp.sum(grad_pre.astype(wide), axis=0)
    grad_normed_two = sum_cols(weigh(grad_pre, w_fc1, True).astype(short)).astype(wide)
    back_two, gain_two, shift_two = norm_backward(
        grad_normed_two, centred_two, scale_two, vectors[3]
    )
    grad_mid = cot_wide + back_two
    grad_mid_short = grad_mid.astype(short)
    grad_bias_proj = jnp.sum(grad_mid_short.astype(wide), axis=0)
    grad_proj_t = lax.dynamic_slice_in_dim(
        outer_sum(grad_mid_short, att_own).astype(short), own_start, part, 1
    )
    shard_proj = reduce_groups(reduce_rows(grad_proj_t), 0)
    grad_att = split_heads(weigh(grad_mid_short, w_proj_t, False).astype(short))
    grad_values = batched("hqk,hqd->hkd", weights, grad_att)
    grad_probs = batched("hqd,hkd->hqk", grad_att, values)
    delta = jnp.sum(grad_att.astype(wide) * attended.astype(wide), axis=2, keepdims=True)
    grad_scores = (probs * (grad_probs - delta) * HD ** (-0.5)).astype(short)
    grad_query = batched("hqk,hkd->hqd", grad_scores, keys)
    grad_keys = batched("hqk,hqd->hkd", grad_scores, queries)
    units = [
        lax.dynamic_slice_in_dim(join_heads(grad.astype(short)), own_start, part, 1)
        for grad in (grad_query, grad_keys, grad_values)
    ]
    grad_ext = jnp.concatenate(
        [
            jnp.where(own[None, :], join_heads(grad.astype(short)), 0).astype(short)
            for grad in (grad_query, grad_keys, grad_values)
        ],
        axis=1,
    )
    stacked = jnp.stack(units)
    picks = [
        lax.dynamic_index_in_dim(stacked, jnp.array(table)[my_col], 0, keepdims=False)
        for table in ((0, 1, 1, 2), (1, 0, 2, 1), (2, 2, 0, 0))
    ]
    unit_b = swap_cols(picks[1], 1)
    unit_c = swap_cols(picks[2], 2)
    grad_block = jnp.concatenate(
        [jnp.where(odd, unit_c, picks[0]), unit_b, jnp.where(odd, picks[0], unit_c)], axis=1
    )
    grad_normed_one = sum_cols(weigh(grad_ext, w_qkv, True).astype(short)).astype(wide)
    grad_qkv = outer_sum(normed_one, grad_block).astype(short)
    shard_qkv = reduce_groups(reduce_rows(grad_qkv), 1)
    grad_bias_qkv = jnp.sum(grad_block.astype(wide), axis=0)
    back_one, gain_one, shift_one = norm_backward(
        grad_normed_one, centred_one, scale_one, vectors[0]
    )
    in_grad = lax.dynamic_slice_in_dim(grad_mid + back_one, my_col * part, part, 1)
    block_in_grad = swap_grid(in_grad.astype(short)).astype(wide)

    row_grads = jnp.stack(
        [gain_one, shift_one, grad_bias_proj, gain_two, shift_two, grad_bias_two]
    )
    sums = lax.psum(
        jnp.concatenate([row_grads.reshape(-1), grad_bias_fc1, grad_bias_qkv]), ("row", "dp")
    )
    vec_size = part // n_dp
    row_shard = lax.dynamic_slice_in_dim(
        sums[: 6 * D].reshape(6, D), my_row * part + my_dp * vec_size, vec_size, 1
    )[:, None, :]
    fc1_bias_shard = lax.dynamic_slice_in_dim(
        sums[6 * D : 6 * D + grad_bias_fc1.shape[0]], my_dp * b1_size, b1_size, 0
    )[None, :]
    qkv_bias_shard = lax.dynamic_slice_in_dim(
        sums[6 * D + grad_bias_fc1.shape[0] :], my_dp * qkv_bias.size, qkv_bias.size, 0
    )[None, :]
    grads = (
        shard_qkv.astype(wide)[:, None, :],
        shard_proj.astype(wide).T[:, None, :],
        shard_fc1.astype(wide)[:, None, :],
        shard_fc2.astype(wide).T[:, None, :],
        qkv_bias_shard,
        fc1_bias_shard,
        row_shard,
    )
    masters = (qkv_weight, proj_weight, fc1_weight, fc2_weight, qkv_bias, fc1_bias, row_vectors)
    moments = (
        qkv_moments,
        proj_moments,
        fc1_moments,
        fc2_moments,
        qkv_bias_moments,
        fc1_bias_moments,
        row_moments,
    )
    decays = (DECAY_RATE, DECAY_RATE, DECAY_RATE, DECAY_RATE, 0.0, 0.0, 0.0)
    rates = (LEARN_RATE, LEARN_RATE, LEARN_RATE, LEARN_RATE, VECTOR_RATE, VECTOR_RATE, VECTOR_RATE)
    updates = [
        adam_step(master, moment, gradient, decay_rate, step_rate)
        for master, moment, gradient, decay_rate, step_rate in zip(
            masters, moments, grads, decays, rates
        )
    ]
    return (
        block_out,
        block_in_grad,
        grads[0],
        grads[1],
        grads[2],
        grads[3],
        grads[4],
        grads[5],
        grads[6],
        updates[0][0],
        updates[1][0],
        updates[2][0],
        updates[3][0],
        updates[4][0],
        updates[5][0],
        updates[6][0],
        updates[0][1],
        updates[1][1],
        updates[2][1],
        updates[3][1],
        updates[4][1],
        updates[5][1],
        updates[6][1],
    )


def solution(mesh):
    in_specs = (
        P(("dp", "col"), "row"),
        P(("dp", "col"), "row"),
        P(("dp", "row"), None),
        P("row", "col", "dp"),
        P("col", "row", "dp"),
        P("row", "col", "dp"),
        P("col", "row", "dp"),
        P("col", "dp"),
        P("col", "dp"),
        P(None, "row", "dp"),
        P(None, "row", "col", "dp"),
        P(None, "col", "row", "dp"),
        P(None, "row", "col", "dp"),
        P(None, "col", "row", "dp"),
        P(None, "col", "dp"),
        P(None, "col", "dp"),
        P(None, None, "row", "dp"),
    )
    out_specs = (
        P(("dp", "col"), "row"),
        P(("dp", "col"), "row"),
        P("row", "col", "dp"),
        P("col", "row", "dp"),
        P("row", "col", "dp"),
        P("col", "row", "dp"),
        P("col", "dp"),
        P("col", "dp"),
        P(None, "row", "dp"),
        P("row", "col", "dp"),
        P("col", "row", "dp"),
        P("row", "col", "dp"),
        P("col", "row", "dp"),
        P("col", "dp"),
        P("col", "dp"),
        P(None, "row", "dp"),
        P(None, "row", "col", "dp"),
        P(None, "col", "row", "dp"),
        P(None, "row", "col", "dp"),
        P(None, "col", "row", "dp"),
        P(None, "col", "dp"),
        P(None, "col", "dp"),
        P(None, None, "row", "dp"),
    )
    return jax.shard_map(
        on_device, mesh=mesh, in_specs=in_specs, out_specs=out_specs, check_vma=False
    )
```

```python
import jax
import jax.numpy as jnp
from jax import lax
from jax.sharding import PartitionSpec as P

D = 1088
H = 17
HD = 64
STEP = 3
EXT = 320
HALO = 48


NORM_EPS = 1e-05
BETA_ONE = 0.9
BETA_TWO = 0.95
LEARN_RATE = 0.05
VECTOR_RATE = 0.2
DECAY_RATE = 0.1
ADAM_EPS = 1e-08


def gelu_tanh(values_in):
    return jax.nn.gelu(values_in, approximate=True)


def weigh(row_block, weight, transposed):
    return lax.dot_general(
        row_block,
        weight,
        (((1,), (1 if transposed else 0,)), ((), ())),
        preferred_element_type=jnp.float32,
    )


def outer_sum(left_rows, right_rows):
    return lax.dot_general(
        left_rows, right_rows, (((0,), (0,)), ((), ())), preferred_element_type=jnp.float32
    )


def swap_grid(block):
    count = lax.axis_size("row")
    pairs = [(r * count + c, c * count + r) for r in range(count) for c in range(count)]
    return lax.ppermute(block, ("row", "col"), pairs)


def row_stats(values_in):
    row_mean = jnp.mean(values_in, axis=1, keepdims=True)
    spread = jnp.mean(values_in * values_in, axis=1, keepdims=True) - row_mean * row_mean
    return row_mean, lax.rsqrt(spread + NORM_EPS)


def norm_backward(upstream, centred, inv_scale, gain_row):
    pushed = upstream * gain_row
    row_total = jnp.mean(pushed, axis=1, keepdims=True)
    cross = jnp.mean(pushed * centred, axis=1, keepdims=True)
    result = inv_scale * (pushed - row_total - centred * cross)
    return (result, jnp.sum(upstream * centred, axis=0), jnp.sum(upstream, axis=0))


def step_right(block, senders):
    return lax.ppermute(block, "row", [(q, q + 1) for q in senders])


def step_left(block, senders):
    return lax.ppermute(block, "row", [(q, q - 1) for q in senders])


def gather_rows(block):
    count = lax.axis_size("row")
    mine = lax.axis_index("row")
    size = block.shape[0]
    from_left, from_right = [], []
    lefts, rights = block, block
    for step in range(1, count):
        lefts = step_right(lefts, range(step - 1, count - 1))
        rights = step_left(rights, range(1, count - step + 1))
        from_left.append(lefts)
        from_right.append(rights)
    whole = jnp.zeros((size * count,) + block.shape[1:], block.dtype)
    whole = lax.dynamic_update_slice_in_dim(whole, block, mine * size, 0)
    for step in range(1, count):
        piece = jnp.where(mine >= step, from_left[step - 1], from_right[count - step - 1])
        place = lax.rem(mine - step + count, count)
        whole = lax.dynamic_update_slice_in_dim(whole, piece, place * size, 0)
    return whole


def reduce_rows(grad, extra=None):
    count = lax.axis_size("row")
    mine = lax.axis_index("row")
    size = grad.shape[0] // count

    def own_block(index):
        block = lax.dynamic_slice_in_dim(grad, jnp.clip(index, 0, count - 1) * size, size, 0)
        if extra is None:
            return block
        return jnp.concatenate([block, extra, pad_rows(extra)], axis=0)

    lefts, rights = None, None
    for step in range(1, count):
        up = own_block(mine + count - step)
        down = own_block(mine - count + step)
        if lefts is not None:
            up = (up.astype(jnp.float32) + lefts.astype(jnp.float32)).astype(grad.dtype)
            down = (down.astype(jnp.float32) + rights.astype(jnp.float32)).astype(grad.dtype)
        lefts = step_right(up, range(step))
        rights = step_left(down, range(count - step, count))
    total = own_block(mine).astype(jnp.float32) + lefts.astype(jnp.float32)
    return (total + rights.astype(jnp.float32)).astype(grad.dtype)


def swap_cols(block, bit):
    return lax.ppermute(block, "col", [(c, c ^ bit) for c in range(lax.axis_size("col"))])


def gather_features(block):
    mine = lax.axis_index("col")
    near = swap_cols(block, 1)
    pair = jnp.stack([block, near])
    both = jnp.concatenate([pair, swap_cols(pair, 2)], axis=0)
    return jnp.concatenate(
        [
            lax.dynamic_index_in_dim(both, mine ^ j, 0, keepdims=False)
            for j in range(lax.axis_size("col"))
        ],
        axis=1,
    )


def sum_cols(part):
    half = part.shape[0] // 2
    side = lax.axis_index("col") % 2
    wide = jnp.float32
    kept = lax.dynamic_slice_in_dim(part, side * half, half, 0)
    sent = lax.dynamic_slice_in_dim(part, (1 - side) * half, half, 0)
    chip = (kept.astype(wide) + swap_cols(sent, 1).astype(wide)).astype(part.dtype)
    both = (chip.astype(wide) + swap_cols(chip, 2).astype(wide)).astype(part.dtype)
    other = swap_cols(both, 1)
    return jnp.where(
        side == 0,
        jnp.concatenate([both, other], axis=0),
        jnp.concatenate([other, both], axis=0),
    )


def gather_groups(block, dim):
    count = lax.axis_size("dp")
    if count != 2:
        return lax.all_gather(block, "dp", axis=dim, tiled=True)
    other = lax.ppermute(block, "dp", [(0, 1), (1, 0)])
    first = lax.axis_index("dp") == 0
    return jnp.where(
        first,
        jnp.concatenate([block, other], axis=dim),
        jnp.concatenate([other, block], axis=dim),
    )


def pad_rows(row):
    return jnp.zeros((15,) + row.shape[1:], row.dtype)


def with_halo(units, own_start):
    count = lax.axis_size("col")
    width = units.shape[-1]
    from_left = lax.ppermute(
        units[..., width - HALO :], "col", [(i, i + 1) for i in range(count - 1)]
    )
    from_right = lax.ppermute(units[..., :HALO], "col", [(i + 1, i) for i in range(count - 1)])
    return lax.dynamic_slice_in_dim(
        jnp.concatenate([from_left, units, from_right], axis=-1),
        HALO - own_start,
        EXT,
        units.ndim - 1,
    )


def reduce_groups(grad, dim):
    count = lax.axis_size("dp")
    if count != 2:
        return lax.psum_scatter(grad, "dp", scatter_dimension=dim, tiled=True)
    half = grad.shape[dim] // 2
    mine = lax.axis_index("dp")
    kept = lax.dynamic_slice_in_dim(grad, mine * half, half, dim)
    sent = lax.dynamic_slice_in_dim(grad, (1 - mine) * half, half, dim)
    return kept.astype(jnp.float32) + lax.ppermute(sent, "dp", [(0, 1), (1, 0)]).astype(jnp.float32)


def split_heads(columns):
    rows = columns.shape[0]
    return columns.reshape(rows, EXT // HD, HD).transpose(1, 0, 2)


def join_heads(heads):
    return heads.transpose(1, 0, 2).reshape(heads.shape[1], EXT)


def batched(spec, left, right):
    return jnp.einsum(spec, left, right, preferred_element_type=jnp.float32)


def adam_step(master, moment, gradient, decay_rate, step_rate):
    first_moment = BETA_ONE * moment[0] + (1.0 - BETA_ONE) * gradient
    second_moment = BETA_TWO * moment[1] + (1.0 - BETA_TWO) * gradient * gradient
    change = (
        first_moment
        / (1.0 - BETA_ONE**STEP)
        / (jnp.sqrt(second_moment / (1.0 - BETA_TWO**STEP)) + ADAM_EPS)
    )
    change = change + decay_rate * master
    return (master - step_rate * change, jnp.stack([first_moment, second_moment]))


def on_device(
    block_in,
    cotangent,
    lengths,
    qkv_weight,
    proj_weight,
    fc1_weight,
    fc2_weight,
    qkv_bias,
    fc1_bias,
    row_vectors,
    qkv_moments,
    proj_moments,
    fc1_moments,
    fc2_moments,
    qkv_bias_moments,
    fc1_bias_moments,
    row_moments,
):
    wide = jnp.float32
    short = jnp.bfloat16
    my_col = lax.axis_index("col")
    n_col = lax.axis_size("col")
    n_row = lax.axis_size("row")
    part = D // n_col
    pack_len = block_in.shape[0]

    x_part = swap_grid(block_in)
    x_bf = gather_features(x_part)
    cot_part = swap_grid(cotangent)
    cot = gather_features(cot_part)

    own_start = my_col * (part - (EXT - HD))
    odd = (my_col % 2) == 1
    qkv_block = gather_groups(
        jnp.concatenate([qkv_weight[:, 0, :], qkv_bias, pad_rows(qkv_bias)], axis=0).astype(short),
        1,
    )
    first_unit, unit_b, last_unit = (qkv_block[:, i * part : (i + 1) * part] for i in range(3))
    arrived = jnp.stack(
        [
            jnp.where(odd, last_unit, first_unit),
            swap_cols(unit_b, 1),
            swap_cols(jnp.where(odd, first_unit, last_unit), 2),
        ]
    )
    qkv_units = jnp.stack(
        [
            lax.dynamic_index_in_dim(arrived, jnp.array(table)[my_col], 0, keepdims=False)
            for table in ((0, 1, 2, 2), (1, 0, 0, 1), (2, 2, 1, 0))
        ]
    )
    qkv_ext = with_halo(qkv_units, own_start)
    bias_qkv = qkv_ext[:, part, :].reshape(-1).astype(wide)
    w_qkv = gather_rows(
        jnp.concatenate([qkv_ext[0, :part], qkv_ext[1, :part], qkv_ext[2, :part]], axis=1)
    )

    proj_t = proj_weight[:, 0, :].astype(short).T
    vectors_t = row_vectors[:, 0, :].astype(short).T
    filler = jnp.zeros((vectors_t.shape[0], 384 - EXT - vectors_t.shape[1]), short)
    proj_all = gather_rows(
        gather_groups(
            jnp.concatenate([with_halo(proj_t, own_start), vectors_t, filler], axis=1), 0
        )
    )
    w_proj_t = proj_all[:, :EXT]
    vectors = proj_all[:, EXT : EXT + 6].astype(wide).T
    fc1_block = gather_groups(
        jnp.concatenate([fc1_weight[:, 0, :], fc1_bias, pad_rows(fc1_bias)], axis=0).astype(short),
        1,
    )
    bias_fc1 = fc1_block[part].astype(wide)
    w_fc1 = gather_rows(fc1_block[:part])
    w_fc2_t = gather_rows(gather_groups(fc2_weight[:, 0, :].astype(short).T, 0))

    x_full = x_bf.astype(wide)
    mean_one, scale_one = row_stats(x_full)
    centred_one = (x_full - mean_one) * scale_one
    normed_one = (centred_one * vectors[0] + vectors[1]).astype(short)
    mixed = (weigh(normed_one, w_qkv, False) + bias_qkv).astype(short)
    queries = split_heads(mixed[:, :EXT])
    keys = split_heads(mixed[:, EXT : 2 * EXT])
    values = split_heads(mixed[:, 2 * EXT :])
    seq_ends = jnp.cumsum(lengths[0])
    places = jnp.arange(pack_len, dtype=jnp.int32)
    segment = jnp.sum((places[:, None] >= seq_ends[None, :]).astype(jnp.int32), axis=1)
    allowed = (segment[:, None] == segment[None, :]) & (places[None, :] <= places[:, None])
    scores = jnp.where(
        allowed[None], batched("hqd,hkd->hqk", queries, keys) * HD ** (-0.5), -1e30
    )
    row_top = jnp.max(scores, axis=2, keepdims=True)
    log_total = row_top + jnp.log(jnp.sum(jnp.exp(scores - row_top), axis=2, keepdims=True))
    probs = jnp.exp(scores - log_total)
    weights = probs.astype(short)
    attended = batched("hqk,hkd->hqd", weights, values).astype(short)
    own = jnp.arange(EXT)
    own = (own >= own_start) & (own < own_start + part)
    att_own = jnp.where(own[None, :], join_heads(attended), 0).astype(short)
    x_mid = (
        x_full
        + sum_cols(weigh(att_own, w_proj_t, True).astype(short)).astype(wide)
        + vectors[2]
    )

    mean_two, scale_two = row_stats(x_mid)
    centred_two = (x_mid - mean_two) * scale_two
    normed_two = (centred_two * vectors[3] + vectors[4]).astype(short)
    pre_act = weigh(normed_two, w_fc1, False) + bias_fc1
    hidden = gelu_tanh(pre_act).astype(short)
    out_part = lax.psum_scatter(
        weigh(hidden, w_fc2_t, True).astype(short), "col", scatter_dimension=1, tiled=True
    ).astype(wide)
    mid_part = lax.dynamic_slice_in_dim(x_mid, my_col * part, part, 1)
    shift_part = lax.dynamic_slice_in_dim(vectors[5], my_col * part, part, 0)
    block_out = swap_grid((mid_part + out_part + shift_part).astype(short))

    grad_hidden = weigh(cot, w_fc2_t, False)
    grad_pre = jax.vjp(gelu_tanh, pre_act)[1](grad_hidden)[0].astype(short)
    grad_fc2_t = outer_sum(cot, hidden).astype(short)
    shard_fc2 = reduce_groups(reduce_rows(grad_fc2_t), 0)
    grad_fc1 = outer_sum(normed_two, grad_pre).astype(short)
    cot_wide = cot.astype(wide)
    grad_bias_two = jnp.sum(cot_wide, axis=0)
    grad_bias_fc1 = jnp.sum(grad_pre.astype(wide), axis=0)
    shard_fc1 = reduce_groups(reduce_rows(grad_fc1, grad_bias_fc1[None, :].astype(short)), 1)
    grad_normed_two = sum_cols(weigh(grad_pre, w_fc1, True).astype(short)).astype(wide)
    back_two, gain_two, shift_two = norm_backward(
        grad_normed_two, centred_two, scale_two, vectors[3]
    )
    grad_mid = cot_wide + back_two
    grad_mid_short = grad_mid.astype(short)
    grad_bias_proj = jnp.sum(grad_mid_short.astype(wide), axis=0)
    grad_proj_t = lax.dynamic_slice_in_dim(
        outer_sum(grad_mid_short, att_own).astype(short), own_start, part, 1
    )
    shard_proj = reduce_groups(reduce_rows(grad_proj_t), 0)
    grad_att = split_heads(weigh(grad_mid_short, w_proj_t, False).astype(short))
    grad_values = batched("hqk,hqd->hkd", weights, grad_att)
    grad_probs = batched("hqd,hkd->hqk", grad_att, values)
    delta = jnp.sum(grad_att.astype(wide) * attended.astype(wide), axis=2, keepdims=True)
    grad_scores = (probs * (grad_probs - delta) * HD ** (-0.5)).astype(short)
    grad_query = batched("hqk,hkd->hqd", grad_scores, keys)
    grad_keys = batched("hqk,hqd->hkd", grad_scores, queries)
    units = [
        lax.dynamic_slice_in_dim(join_heads(grad.astype(short)), own_start, part, 1)
        for grad in (grad_query, grad_keys, grad_values)
    ]
    grad_ext = jnp.concatenate(
        [
            jnp.where(own[None, :], join_heads(grad.astype(short)), 0).astype(short)
            for grad in (grad_query, grad_keys, grad_values)
        ],
        axis=1,
    )
    stacked = jnp.stack(units)
    picks = [
        lax.dynamic_index_in_dim(stacked, jnp.array(table)[my_col], 0, keepdims=False)
        for table in ((0, 1, 1, 2), (1, 0, 2, 1), (2, 2, 0, 0))
    ]
    unit_b = swap_cols(picks[1], 1)
    unit_c = swap_cols(picks[2], 2)
    grad_block = jnp.concatenate(
        [jnp.where(odd, unit_c, picks[0]), unit_b, jnp.where(odd, picks[0], unit_c)], axis=1
    )
    grad_normed_one = sum_cols(weigh(grad_ext, w_qkv, True).astype(short)).astype(wide)
    grad_qkv = outer_sum(normed_one, grad_block).astype(short)
    grad_bias_qkv = jnp.sum(grad_block.astype(wide), axis=0)
    shard_qkv = reduce_groups(reduce_rows(grad_qkv, grad_bias_qkv[None, :].astype(short)), 1)
    back_one, gain_one, shift_one = norm_backward(
        grad_normed_one, centred_one, scale_one, vectors[0]
    )
    in_grad = lax.dynamic_slice_in_dim(grad_mid + back_one, my_col * part, part, 1)
    block_in_grad = swap_grid(in_grad.astype(short)).astype(wide)

    nothing = jnp.zeros_like(gain_one)
    row_grads = jnp.stack(
        [gain_one, shift_one, grad_bias_proj, gain_two, shift_two, grad_bias_two, nothing, nothing]
    )
    row_blocks = row_grads.reshape(8, n_row, part).transpose(1, 0, 2).reshape(8 * n_row, part)
    row_shard = reduce_groups(reduce_rows(row_blocks), 1)[:6, None, :].astype(wide)
    grads = (
        shard_qkv.astype(wide)[:part, None, :],
        shard_proj.astype(wide).T[:, None, :],
        shard_fc1.astype(wide)[:part, None, :],
        shard_fc2.astype(wide).T[:, None, :],
        shard_qkv.astype(wide)[part : part + 1],
        shard_fc1.astype(wide)[part : part + 1],
        row_shard,
    )
    masters = (qkv_weight, proj_weight, fc1_weight, fc2_weight, qkv_bias, fc1_bias, row_vectors)
    moments = (
        qkv_moments,
        proj_moments,
        fc1_moments,
        fc2_moments,
        qkv_bias_moments,
        fc1_bias_moments,
        row_moments,
    )
    decays = (DECAY_RATE, DECAY_RATE, DECAY_RATE, DECAY_RATE, 0.0, 0.0, 0.0)
    rates = (LEARN_RATE, LEARN_RATE, LEARN_RATE, LEARN_RATE, VECTOR_RATE, VECTOR_RATE, VECTOR_RATE)
    updates = [
        adam_step(master, moment, gradient, decay_rate, step_rate)
        for master, moment, gradient, decay_rate, step_rate in zip(
            masters, moments, grads, decays, rates
        )
    ]
    return (
        block_out,
        block_in_grad,
        grads[0],
        grads[1],
        grads[2],
        grads[3],
        grads[4],
        grads[5],
        grads[6],
        updates[0][0],
        updates[1][0],
        updates[2][0],
        updates[3][0],
        updates[4][0],
        updates[5][0],
        updates[6][0],
        updates[0][1],
        updates[1][1],
        updates[2][1],
        updates[3][1],
        updates[4][1],
        updates[5][1],
        updates[6][1],
    )


def solution(mesh):
    in_specs = (
        P(("dp", "col"), "row"),
        P(("dp", "col"), "row"),
        P(("dp", "row"), None),
        P("row", "col", "dp"),
        P("col", "row", "dp"),
        P("row", "col", "dp"),
        P("col", "row", "dp"),
        P("col", "dp"),
        P("col", "dp"),
        P(None, "row", "dp"),
        P(None, "row", "col", "dp"),
        P(None, "col", "row", "dp"),
        P(None, "row", "col", "dp"),
        P(None, "col", "row", "dp"),
        P(None, "col", "dp"),
        P(None, "col", "dp"),
        P(None, None, "row", "dp"),
    )
    out_specs = (
        P(("dp", "col"), "row"),
        P(("dp", "col"), "row"),
        P("row", "col", "dp"),
        P("col", "row", "dp"),
        P("row", "col", "dp"),
        P("col", "row", "dp"),
        P("col", "dp"),
        P("col", "dp"),
        P(None, "row", "dp"),
        P("row", "col", "dp"),
        P("col", "row", "dp"),
        P("row", "col", "dp"),
        P("col", "row", "dp"),
        P("col", "dp"),
        P("col", "dp"),
        P(None, "row", "dp"),
        P(None, "row", "col", "dp"),
        P(None, "col", "row", "dp"),
        P(None, "row", "col", "dp"),
        P(None, "col", "row", "dp"),
        P(None, "col", "dp"),
        P(None, "col", "dp"),
        P(None, None, "row", "dp"),
    )
    return jax.shard_map(
        on_device, mesh=mesh, in_specs=in_specs, out_specs=out_specs, check_vma=False
    )
```
